256 devices in a mesh: pgroup: 2 (over core), code: 4 (over x), vrow: 32 (over z, y).
Axes of the slice: x: 4, y: 4, z: 8, core: 2. Of those that a mesh axis runs over, the one named last changes fastest.
Arguments:
- tile_values: bfloat16 [131072, 4096], P(('pgroup', 'vrow'), 'code'), may hold values from -6 to 6
- tile_block: int32 [1024, 32], P(('pgroup', 'vrow'), 'code'), may hold values from 0 to 159, as said below
- visit_counts: int32 [1024, 4], P(('pgroup', 'vrow')), may hold values from 1 to 96, 128 in all within a row
- code_factor: bfloat16 [20480, 256], P('code'), may hold values from 0 to 0.014953613
- slice_mix: float32 [256, 256], replicated, may hold values from 0 to 0.125
- patient_weight: float32 [4096, 256], P(('pgroup', 'vrow')), may hold values from 0.5 to 1.5
Outputs:
- visit_factor: float32 [131072, 256], P(('pgroup', 'vrow'))
- slice_mix_new: float32 [256, 256], replicated
- weight_new: float32 [4096, 256], P(('pgroup', 'vrow'))
The draws below stay inside these ranges and needn't reach their ends.
Inputs may be any that keep to these rules, and one draw needn't show every extreme that they name: `tile_block`: column t of a window names a block of 128 codes lying within codes s * 5120 to s * 5120 + 5119, where s = (t // 2) % 4. `visit_counts`: the counts of each window sum to 128; in every window one patient has exactly 96 visits.
All inputs are finite; a program needn't handle non-finite values.
Results may differ from the reference program's by a relative error of at most 0.0003.
Values may be sent and summed in bfloat16 or wider, within the bound.
No kernel may reach another device: no remote copies, remote signals or barrier semaphores. Data moves between devices by JAX's collectives and lax.ppermute only.
A program may use at most 128 MiB of HBM per device.

```python
import math
import jax
import jax.numpy as jnp
import numpy as np
from jax import lax

TILE = 128
R = 256
J_DEV = 5120
PAT_WIN = 4
TPS = 2
NS_ITERS = 5
NNLS_ITERS = 4
J = 20480
TILES_ROW = 32
WINDOWS = 1024
ROWS = 131072
PATIENTS = 4096
N_CODE = 4


def draw_tile_block(key, part):
    key = jax.random.fold_in(key, 17)
    code_blocks = J_DEV // TILE
    column = jnp.arange(TILES_ROW, dtype=jnp.int32)
    owner = column // TPS % N_CODE
    offset = jax.random.randint(key, (WINDOWS, TILES_ROW), 0, code_blocks)
    return (owner[None, :] * code_blocks + offset).astype(jnp.int32)


def block_levels(key, shape, shards, smallest, largest):
    loudness = 1.0
    for dim, parts in shards:
        draws = jax.random.uniform(jax.random.fold_in(jax.random.fold_in(key, 6), dim), (parts,), jnp.float32, smallest / len(shards), largest / len(shards))
        loudness = loudness * jnp.repeat(jnp.exp(draws), shape[dim] // parts).reshape((-1,) + (1,) * (len(shape) - 1 - dim))
    return loudness


def profile(amount, total, reach, skew):
    loads = [(1 << 20) // math.isqrt(standing ** skew) + 1 for standing in range(2, amount + 1)]
    surplus, holding = total - reach - (amount - 1), [1] * (amount - 1)
    while surplus > 0:
        movable = [i for i in range(amount - 1) if holding[i] < reach]
        mass, budget = sum([loads[i] for i in movable]), surplus
        for i in movable:
            extra = min(reach - holding[i], max(1, budget * loads[i] // mass), surplus)
            holding[i] = holding[i] + extra
            surplus = surplus - extra
    return np.array([reach] + holding)


def uneven(own_key, amount, total, most, lean):
    if amount == 2:
        one = jax.random.randint(own_key, (), max(1, total - most), min(most, total - 1) + 1)
        return jnp.stack([one, total - one])
    lengths = jnp.asarray(profile(amount, total, most, lean), jnp.int32)
    pairs = (amount - 1) // 2
    source_of, receiver = lengths[1:1 + 2 * pairs:2], lengths[2:2 + 2 * pairs:2]
    room = jnp.minimum(source_of - 1, most - receiver)
    passed = jax.random.randint(jax.random.fold_in(own_key, 1), (pairs,), 0, 1 << 20) % (room + 1)
    lengths = lengths.at[1:1 + 2 * pairs:2].set(source_of - passed).at[2:2 + 2 * pairs:2].set(receiver + passed)
    return lengths[jax.random.permutation(jax.random.fold_in(own_key, 2), amount)]


def scatter_about(rng, shape, spread, reach, shards=(), kind=jnp.bfloat16):
    level = block_levels(rng, shape, shards, -0.22, 0.18) if shards else 1.0
    entries = jax.random.normal(rng, shape, jnp.float32) * spread * level
    return jnp.minimum(jnp.maximum(entries, -reach), reach).astype(kind)


def setup_inputs(seed: int = 0) -> dict:
    seeds = jax.random.split(jax.random.key(seed), 7)
    return {
        "tile_values": scatter_about(seeds[0], (ROWS, TILES_ROW * TILE), 1.0, 6.0, ((0, 64), (1, 4))),
        "tile_block": draw_tile_block(jax.random.fold_in(seeds[6], 71), 0),
        "visit_counts": jax.vmap(lambda own: uneven(own, PAT_WIN, TILE, 3 * TILE // 4, 2))(jax.random.split(seeds[2], WINDOWS)).reshape((WINDOWS, PAT_WIN)).astype(jnp.int32),
        "code_factor": jnp.clip(0.014953613 * jax.random.uniform(seeds[3], (J, R), jnp.float32) ** block_levels(seeds[3], (J, R), ((0, 4),), -0.2, 0.2), 0.0, 0.014953613).astype(jnp.bfloat16),
        "slice_mix": jnp.clip(jax.random.uniform(seeds[4], (R, R), jnp.float32, 0.0, 0.125), 0.0, 0.125),
        "patient_weight": jnp.clip(0.5 + 1.0 * jax.random.uniform(seeds[5], (PATIENTS, R), jnp.float32) ** block_levels(seeds[5], (PATIENTS, R), ((0, 64),), -0.2, 0.2), 0.5, 1.5),
    }


EPSILON = 1e-06
PRECISE = lax.Precision.HIGHEST

def reference(tile_values, tile_block, visit_counts, code_factor, slice_mix, patient_weight):
    rank_cols = code_factor.shape[1]
    windows = tile_values.shape[0] // TILE
    tile_view = tile_values.astype(jnp.float32).reshape(windows, TILE, TILES_ROW, TILE)
    factor_view = code_factor.astype(jnp.float32).reshape(J // TILE, TILE, rank_cols)

    def one_window(item):
        rows_here, block_ids = item
        chosen = factor_view[block_ids.astype(jnp.int32)]
        return jnp.einsum('atc,tcr->ar', rows_here, chosen, precision=PRECISE)
    projected = lax.map(one_window, (tile_view, tile_block))
    counts = visit_counts.astype(jnp.int32)
    starts = jnp.cumsum(counts, axis=1) - counts
    position = jnp.arange(TILE, dtype=jnp.int32)
    inside = (position[None, :, None] >= starts[:, None, :]) & (position[None, :, None] < (starts + counts)[:, None, :])
    member = inside.astype(jnp.float32)
    weights = patient_weight.reshape(windows, PAT_WIN, rank_cols)
    row_weight = jnp.einsum('wip,wpr->wir', member, weights, precision=PRECISE)
    scaled = projected * row_weight
    mixed_rows = jnp.einsum('wir,sr->wis', scaled, slice_mix, precision=PRECISE)
    squares = jnp.einsum('wip,wi->wp', member, lax.optimization_barrier(jnp.sum(mixed_rows * mixed_rows, axis=2)), precision=PRECISE)
    row_norm = jnp.einsum('wip,wp->wi', member, squares, precision=PRECISE)
    factor = mixed_rows / jnp.sqrt(row_norm + EPSILON)[:, :, None]
    same_patient = jnp.einsum('wip,wjp->wij', member, member, precision=PRECISE)
    for repeat in range(NS_ITERS):
        gram_rows = jnp.einsum('wir,wjr->wij', factor, factor, precision=PRECISE) * same_patient
        factor = 1.5 * factor - 0.5 * jnp.einsum('wij,wjr->wir', gram_rows, factor, precision=PRECISE)
    code_gram = jnp.dot(code_factor.T, code_factor, preferred_element_type=jnp.float32)
    weight_gram = jnp.dot(patient_weight.T, patient_weight, precision=PRECISE)
    target = jnp.einsum('wir,wis->rs', factor, scaled, precision=PRECISE)
    curvature = weight_gram * code_gram
    step_scale = jnp.sqrt(jnp.sum(curvature * curvature))
    mixing = slice_mix
    for repeat in range(NNLS_ITERS):
        mixing = jnp.maximum(mixing - (jnp.dot(mixing, curvature, precision=PRECISE) - target) / step_scale, 0.0)
    turned = jnp.einsum('wir,rs->wis', factor, mixing, precision=PRECISE)
    weight_terms = jnp.einsum('wip,wir->wpr', member, projected * turned, precision=PRECISE).reshape(windows * PAT_WIN, rank_cols)
    second = jnp.dot(mixing.T, mixing, precision=PRECISE) * code_gram
    second_scale = jnp.sqrt(jnp.sum(second * second))
    weight = patient_weight
    for repeat in range(NNLS_ITERS):
        weight = jnp.maximum(weight - (jnp.dot(weight, second, precision=PRECISE) - weight_terms) / second_scale, 0.0)
    visit_factor = factor.reshape(windows * TILE, rank_cols)
    return (visit_factor, mixing, weight)
```

```python
import functools

import jax
import jax.numpy as jnp
from jax import lax
from jax.experimental import pallas as pl
from jax.experimental.pallas import tpu as pltpu
from jax.sharding import PartitionSpec as P

TILE = 128
RANK = 256
NS_ITERS = 5
NNLS_ITERS = 4
N_CODE = 4
CHUNK = 4
CROWS = CHUNK * TILE
EPSILON = 1e-06
F32 = jnp.float32
BF16 = jnp.bfloat16
SMEM = pltpu.SMEM
VMEM = pltpu.VMEM


def shift(x, axis, n, step):
    return lax.ppermute(x, axis, [(i, (i + step) % n) for i in range(n)])


def dg(a, b, ca, cb):
    return lax.dot_general(a, b, (((ca,), (cb,)), ((), ())), preferred_element_type=F32)


def split(a):
    high = a.astype(BF16)
    return high, (a - high.astype(F32)).astype(BF16)


def dot3(a, b, ca=1, cb=0):
    ah, al = a if isinstance(a, tuple) else split(a)
    bh, bl = b if isinstance(b, tuple) else split(b)
    return dg(ah, bh, ca, cb) + (dg(ah, bl, ca, cb) + dg(al, bh, ca, cb))


def patients_of(counts_ref, window):
    e0 = counts_ref[window, 0]
    e1 = e0 + counts_ref[window, 1]
    e2 = e1 + counts_ref[window, 2]
    down = lax.broadcasted_iota(jnp.int32, (TILE, 1), 0)
    along = lax.broadcasted_iota(jnp.int32, (1, TILE), 1)

    def number(i):
        return (i >= e0).astype(jnp.int32) + (i >= e1).astype(jnp.int32) + (i >= e2).astype(jnp.int32)

    return number(down), number(along)


def project_kernel(me_ref, ids_ref, own_ref, r1_ref, r2_ref, r3_ref, factor_ref, out_ref, *, steps):
    me = me_ref[0]
    g = pl.program_id(0)
    step = steps[0]
    for k in range(1, len(steps)):
        step = jnp.where(g == k, steps[k], step)
    chunk = lax.rem(me + step, N_CODE)
    for i in range(CHUNK):
        window = chunk * CHUNK + i
        rows = pl.ds(i * TILE, TILE)
        total = None
        for s, ref in enumerate((own_ref, r1_ref, r2_ref, r3_ref)):
            blocks = []
            for j in range(2):
                at = pl.multiple_of(ids_ref[s * 32 + window * 2 + j] * TILE, TILE)
                blocks.append(factor_ref[pl.ds(at, TILE), :])
            part = dg(ref[rows, :], jnp.concatenate(blocks, axis=0), 1, 0)
            total = part if total is None else total + part
        out_ref[rows, :] = total


def project(me, ids, tiles, received, factor, steps):
    def chunk_of(g, me_ref):
        step = steps[0]
        for k in range(1, len(steps)):
            step = jnp.where(g == k, steps[k], step)
        return lax.rem(me_ref[0] + step, N_CODE)

    n = len(steps)
    return pl.pallas_call(
        functools.partial(project_kernel, steps=steps),
        grid_spec=pltpu.PrefetchScalarGridSpec(
            num_scalar_prefetch=2,
            grid=(n,),
            in_specs=[pl.BlockSpec((CROWS, RANK), lambda g, m, d: (chunk_of(g, m), m[0]))]
            + [pl.BlockSpec((CROWS, RANK), lambda g, m, d: (chunk_of(g, m), 0))] * 3
            + [pl.BlockSpec(factor.shape, lambda g, m, d: (0, 0))],
            out_specs=pl.BlockSpec((CROWS, RANK), lambda g, m, d: (g, 0)),
        ),
        out_shape=jax.ShapeDtypeStruct((n * CROWS, RANK), F32),
        compiler_params=pltpu.CompilerParams(vmem_limit_bytes=40 * 1024 * 1024),
        cost_estimate=pl.CostEstimate(flops=n * CROWS * 1024 * RANK * 2, bytes_accessed=n * 1572864 + 2621440, transcendentals=0),
    )(me, ids, tiles, *received, factor)


def window_kernel(me_ref, counts_ref, p0_ref, p1_ref, p2_ref, weight_ref, mix_ref, proj_ref, q_ref, target_ref):
    me = me_ref[0]
    mix = split(mix_ref[...])
    pids, masks, scaled, factor = [], [], [], []
    for i in range(CHUNK):
        rows = pl.ds(i * TILE, TILE)
        down, along = patients_of(counts_ref, me * CHUNK + i)
        projected = p0_ref[rows, :] + p1_ref[rows, :] + p2_ref[rows, :]
        proj_ref[rows, :] = projected
        w = [weight_ref[pl.ds(i * 4 + p, 1), :] for p in range(4)]
        row_weight = jnp.where(down == 0, w[0], jnp.where(down == 1, w[1], jnp.where(down == 2, w[2], w[3])))
        pids.append(down)
        masks.append(down == along)
        scaled.append(projected * row_weight)
    scaled_split = [split(s) for s in scaled]
    for i in range(CHUNK):
        mixed = dot3(scaled_split[i], mix, 1, 1)
        squares = jnp.sum(mixed * mixed, axis=1, keepdims=True)
        down = pids[i]
        norm = jnp.zeros_like(squares)
        for p in range(4):
            here = down == p
            total = jnp.sum(jnp.where(here, squares, 0.0), axis=0, keepdims=True)
            norm = jnp.where(here, total, norm)
        factor.append(mixed / jnp.sqrt(norm + EPSILON))
    for _ in range(NS_ITERS):
        halves = [split(f) for f in factor]
        gram = [jnp.where(masks[i], dot3(halves[i], halves[i], 1, 1), 0.0) for i in range(CHUNK)]
        for i in range(CHUNK):
            gh, gl = split(gram[i])
            qh, ql = halves[i]
            moved = dg(jnp.concatenate([gh, gl], axis=1), jnp.concatenate([qh, qh], axis=0), 1, 0) + dg(gh, ql, 1, 0)
            factor[i] = 1.5 * factor[i] - 0.5 * moved
    target = None
    for i in range(CHUNK):
        q_ref[pl.ds(i * TILE, TILE), :] = factor[i]
        part = dot3(factor[i], scaled_split[i], 0, 0)
        target = part if target is None else target + part
    target_ref[...] = target


def window_phase(me, counts, parts, weights, mix):
    whole = pl.BlockSpec(memory_space=VMEM)
    smem = pl.BlockSpec(memory_space=SMEM)
    block = jax.ShapeDtypeStruct((CROWS, RANK), F32)
    return pl.pallas_call(
        window_kernel,
        in_specs=[smem, smem] + [whole] * 5,
        out_specs=[whole] * 3,
        out_shape=[block, block, jax.ShapeDtypeStruct((RANK, RANK), F32)],
        compiler_params=pltpu.CompilerParams(vmem_limit_bytes=40 * 1024 * 1024),
        cost_estimate=pl.CostEstimate(flops=10**9, bytes_accessed=4 * 10**6, transcendentals=0),
    )(me, counts, *parts, weights, mix)


def tail_kernel(me_ref, counts_ref, target_ref, wgram_ref, cgram_ref, mix_ref, q_ref, proj_ref, weight_ref,
                g1_ref, g2_ref, g3_ref, mix_out, weight_out, factor_out, sems):
    me = me_ref[0]
    copies = []
    for s, ref in enumerate((g1_ref, g2_ref, g3_ref)):
        at = pl.multiple_of(lax.rem(me + 3 - s, N_CODE) * CROWS, CROWS)
        copies.append(pltpu.make_async_copy(ref, factor_out.at[pl.ds(at, CROWS), :], sems.at[s]))
    copies.append(pltpu.make_async_copy(q_ref, factor_out.at[pl.ds(pl.multiple_of(me * CROWS, CROWS), CROWS), :], sems.at[3]))
    for copy in copies:
        copy.start()
    target = target_ref[...]
    code_gram = cgram_ref[...]
    curvature = wgram_ref[...] * code_gram
    scale = jnp.sqrt(jnp.sum(curvature * curvature, keepdims=True))
    curved = split(curvature)
    mixing = mix_ref[...]
    for _ in range(NNLS_ITERS):
        mixing = jnp.maximum(mixing - (dot3(mixing, curved) - target) / scale, 0.0)
    mix_out[...] = mixing
    halves = split(mixing)
    second = dot3(halves, halves, 0, 0) * code_gram
    second_scale = jnp.sqrt(jnp.sum(second * second, keepdims=True))
    terms = []
    for i in range(CHUNK):
        rows = pl.ds(i * TILE, TILE)
        down, _ = patients_of(counts_ref, me * CHUNK + i)
        product = proj_ref[rows, :] * dot3(q_ref[rows, :], halves)
        for p in range(4):
            terms.append(jnp.sum(jnp.where(down == p, product, 0.0), axis=0, keepdims=True))
    terms = jnp.concatenate(terms, axis=0)
    seconds = split(second)
    weight = weight_ref[...]
    for _ in range(NNLS_ITERS):
        weight = jnp.maximum(weight - (dot3(weight, seconds) - terms) / second_scale, 0.0)
    weight_out[...] = weight
    for copy in copies:
        copy.wait()


def tail_phase(me, counts, target, wgram, cgram, mix, q, proj, weights, gathered):
    whole = pl.BlockSpec(memory_space=VMEM)
    smem = pl.BlockSpec(memory_space=SMEM)
    anywhere = pl.BlockSpec(memory_space=pl.ANY)
    return pl.pallas_call(
        tail_kernel,
        in_specs=[smem, smem] + [whole] * 7 + [anywhere] * 3,
        out_specs=[whole, whole, anywhere],
        out_shape=[
            jax.ShapeDtypeStruct((RANK, RANK), F32),
            jax.ShapeDtypeStruct((CHUNK * 4, RANK), F32),
            jax.ShapeDtypeStruct((N_CODE * CROWS, RANK), F32),
        ],
        scratch_shapes=[pltpu.SemaphoreType.DMA((4,))],
        compiler_params=pltpu.CompilerParams(vmem_limit_bytes=40 * 1024 * 1024),
        cost_estimate=pl.CostEstimate(flops=10**9, bytes_accessed=4 * 10**6, transcendentals=0),
    )(me, counts, target, wgram, cgram, mix, q, proj, weights, *gathered)


def all_sum(x, p):
    half = RANK // 2
    kept = lax.dynamic_slice_in_dim(x, p * half, half, 0)
    passed = lax.dynamic_slice_in_dim(x, (1 - p) * half, half, 0)
    mine = kept + shift(passed, "pgroup", 2, 1)
    spread = ("code", "vrow")
    row = jnp.sum(lax.all_to_all(mine[:, None, :], spread, 0, 0, tiled=True), axis=0)
    rows = jnp.broadcast_to(row[None], (half, 1, x.shape[1]))
    mine = lax.all_to_all(rows, spread, 0, 0, tiled=True)[:, 0, :]
    other = shift(mine, "pgroup", 2, 1)
    return jnp.where(p == 0, jnp.concatenate([mine, other], 0), jnp.concatenate([other, mine], 0))


def local(tile_values, tile_block, visit_counts, code_factor, slice_mix, patient_weight):
    c = lax.axis_index("code")
    p = lax.axis_index("pgroup")
    pv = p * 32 + lax.axis_index("vrow")
    me = jnp.reshape(c, (1,)).astype(jnp.int32)
    windows = tile_block.shape[0]
    first_block = c * (code_factor.shape[0] // TILE)

    def tiles_for(step):
        owner = (c + step) % N_CODE
        values = lax.dynamic_slice_in_dim(tile_values, owner * RANK, RANK, 1)
        numbers = lax.dynamic_slice_in_dim(tile_block, owner * 2, 2, 1).astype(BF16)
        return jnp.concatenate([values, jnp.pad(numbers, ((0, 0), (0, RANK - 2)))], axis=0)

    received = [shift(tiles_for(s), "code", N_CODE, s) for s in (1, 3, 2)]
    received = [received[0], received[2], received[1]]
    own_numbers = lax.dynamic_slice_in_dim(tile_block, c * 2, 2, 1)
    numbers = [own_numbers] + [r[windows * TILE :, :2].astype(jnp.int32) for r in received]
    blocks = code_factor.shape[0] // TILE
    ids = jnp.clip(jnp.stack(numbers).reshape(-1) - first_block, 0, blocks - 1)

    share = code_factor.shape[0] // 64
    code_rows = lax.dynamic_slice_in_dim(code_factor, pv * share, share, 0)
    code_part = lax.dot_general(code_rows, code_rows, (((0,), (0,)), ((), ())), preferred_element_type=F32)
    my_weights = lax.dynamic_slice_in_dim(patient_weight, c * 16, 16, 0)
    weight_part = lax.dot_general(my_weights, my_weights, (((0,), (0,)), ((), ())), precision=lax.Precision.HIGHEST)
    grams = all_sum(jnp.concatenate([weight_part, code_part], axis=1), p)

    far = project(me, ids, tile_values, received, code_factor, (2,))
    up = shift(far[: CROWS // 2], "code", N_CODE, 1)
    down = shift(far[CROWS // 2 :], "code", N_CODE, 3)
    near = project(me, ids, tile_values, received, code_factor, (1, 3, 0))
    half = CROWS // 2
    right = jnp.concatenate([near[:half] + up, near[half:CROWS]], axis=0)
    left = jnp.concatenate([near[CROWS : CROWS + half], near[CROWS + half : 2 * CROWS] + down], axis=0)
    parts = (near[2 * CROWS :], shift(right, "code", N_CODE, 1), shift(left, "code", N_CODE, 3))

    proj, q, target_part = window_phase(me, visit_counts, parts, my_weights, slice_mix)
    gathered = [shift(q, "code", N_CODE, s) for s in (1, 2, 3)]
    target = all_sum(target_part, p)
    mixing, weight, factor = tail_phase(
        me, visit_counts, target, grams[:, :RANK], grams[:, RANK:], slice_mix, q, proj, my_weights, gathered
    )
    others = [shift(weight, "code", N_CODE, s) for s in (1, 2, 3)]
    turned = jnp.stack([weight] + others)
    order = (c - jnp.arange(N_CODE)) % N_CODE
    weight_new = turned[order].reshape(patient_weight.shape)
    return (factor, mixing, weight_new)


def solution(mesh):
    placed = (
        P(("pgroup", "vrow"), "code"),
        P(("pgroup", "vrow"), "code"),
        P(("pgroup", "vrow"), None),
        P("code", None),
        P(),
        P(("pgroup", "vrow"), None),
    )
    return jax.shard_map(
        local,
        mesh=mesh,
        in_specs=placed,
        out_specs=(P(("pgroup", "vrow"), None), P(), P(("pgroup", "vrow"), None)),
        check_vma=False,
    )
```

```python
import functools

import jax
import jax.numpy as jnp
from jax import lax
from jax.experimental import pallas as pl
from jax.experimental.pallas import tpu as pltpu
from jax.sharding import PartitionSpec as P

TILE = 128
RANK = 256
NS_ITERS = 5
NNLS_ITERS = 4
N_CODE = 4
CHUNK = 4
CROWS = CHUNK * TILE
EPSILON = 1e-06
F32 = jnp.float32
BF16 = jnp.bfloat16
SMEM = pltpu.SMEM
VMEM = pltpu.VMEM
BIG = 60 * 1024 * 1024


def shift(x, axis, n, step):
    return lax.ppermute(x, axis, [(i, (i + step) % n) for i in range(n)])


def dg(a, b, ca, cb):
    return lax.dot_general(a, b, (((ca,), (cb,)), ((), ())), preferred_element_type=F32)


def split(a):
    high = a.astype(BF16)
    return high, (a - high.astype(F32)).astype(BF16)


def dot3(a, b, ca=1, cb=0):
    ah, al = a if isinstance(a, tuple) else split(a)
    bh, bl = b if isinstance(b, tuple) else split(b)
    return dg(ah, bh, ca, cb) + (dg(ah, bl, ca, cb) + dg(al, bh, ca, cb))


def patients_of(counts_ref, window):
    e0 = counts_ref[window, 0]
    e1 = e0 + counts_ref[window, 1]
    e2 = e1 + counts_ref[window, 2]
    down = lax.broadcasted_iota(jnp.int32, (TILE, 1), 0)
    along = lax.broadcasted_iota(jnp.int32, (1, TILE), 1)

    def number(i):
        return (i >= e0).astype(jnp.int32) + (i >= e1).astype(jnp.int32) + (i >= e2).astype(jnp.int32)

    return number(down), number(along)


def pack_kernel(me_ref, tiles_ref, block_ref, first_ref, up_ref, down_ref, held, sems):
    rows, spare = tiles_ref.shape[0], block_ref.shape[0]
    half = rows // 2
    fetch = []
    for k, step in enumerate((1, 3)):
        at = pl.multiple_of(lax.rem(me_ref[0] + step, N_CODE) * RANK, RANK)
        for j in range(2):
            here = pl.ds(j * half, half)
            fetch.append(pltpu.make_async_copy(tiles_ref.at[here, pl.ds(at, RANK)], held.at[k, here, :], sems.at[k, j]))
    for copy in fetch:
        copy.start()
    width = block_ref.shape[1]
    place = lax.broadcasted_iota(jnp.int32, (width, RANK), 0) == lax.broadcasted_iota(jnp.int32, (width, RANK), 1)
    numbers = dg(block_ref[...].astype(F32).astype(BF16), jnp.where(place, 1.0, 0.0).astype(BF16), 1, 0).astype(BF16)
    send = []
    for k, ref in enumerate((up_ref, down_ref)):
        held[k, pl.ds(rows, spare), :] = numbers
        for j, size in enumerate((half, half + spare)):
            here = pl.ds(j * half, size)
            send.append(pltpu.make_async_copy(held.at[k, here, :], ref.at[here, :], sems.at[k, 2 + j]))
    for arrived, copy in zip(fetch, send):
        arrived.wait()
        copy.start()
    for copy in send:
        copy.wait()


def pack(me, tiles, block, first):
    whole = pl.BlockSpec(memory_space=VMEM)
    rows = tiles.shape[0] + block.shape[0]
    return pl.pallas_call(
        pack_kernel,
        in_specs=[pl.BlockSpec(memory_space=SMEM), pl.BlockSpec(memory_space=pltpu.HBM), whole, pl.BlockSpec(memory_space=pl.ANY)],
        out_specs=[pl.BlockSpec(memory_space=pl.ANY)] * 2,
        out_shape=[jax.ShapeDtypeStruct((rows, RANK), BF16)] * 2,
        scratch_shapes=[pltpu.VMEM((2, rows, RANK), BF16), pltpu.SemaphoreType.DMA((2, 4))],
        compiler_params=pltpu.CompilerParams(vmem_limit_bytes=BIG),
        cost_estimate=pl.CostEstimate(flops=0, bytes_accessed=4 * 10**6, transcendentals=0),
    )(me, tiles, block, first)


def pair(factor_ref, at):
    return jnp.concatenate([factor_ref[pl.ds(pl.multiple_of(x * TILE, TILE), TILE), :] for x in at], axis=0)


def project_kernel(me_ref, block_ref, ids_ref, tiles_ref, r1_ref, r3_ref, factor_ref, *refs, steps):
    n = len(steps)
    pieces, outs = refs[:8], refs[8 : 8 + 2 * n]
    factor, held, raw, wide, listed, sems, chunk_sems = refs[8 + 2 * n :]
    me = me_ref[0]
    rows = tiles_ref.shape[0]
    spare = r1_ref.shape[0] - rows
    local_rows = factor_ref.shape[0]
    blocks = local_rows // TILE
    piece = pieces[0].shape[0]
    opposite = lax.rem(me + 2, N_CODE)
    numbers = [pltpu.make_async_copy(r.at[pl.ds(rows, spare), :], raw.at[k], sems.at[k]) for k, r in enumerate((r1_ref, r3_ref))]
    tables = [pltpu.make_async_copy(factor_ref, factor.at[pl.ds(0, local_rows), :], sems.at[2])]
    for k, ref in enumerate(pieces):
        tables.append(pltpu.make_async_copy(ref, factor.at[pl.ds(local_rows + k * piece, piece), :], sems.at[3 + k]))
    chunks = []
    for k, step in enumerate(steps):
        here = pl.ds(pl.multiple_of(lax.rem(me + step, N_CODE) * CROWS, CROWS), CROWS)
        sources = [tiles_ref.at[here, pl.ds(pl.multiple_of(x * RANK, RANK), RANK)] for x in (me, opposite)]
        sources += [r1_ref.at[here, :], r3_ref.at[here, :]]
        chunks.append([pltpu.make_async_copy(x, held.at[k, j], chunk_sems.at[k, j]) for j, x in enumerate(sources)])
    for copy in numbers + tables + sum(chunks, []):
        copy.start()
    for copy in numbers:
        copy.wait()
    for k in range(2):
        wide[pl.ds(k * spare, spare), :] = raw[k, :, 0:TILE].astype(F32).astype(jnp.int32)
    down = pltpu.make_async_copy(wide, listed, sems.at[11])
    down.start()
    for copy in tables:
        copy.wait()
    down.wait()
    for k, step in enumerate(steps):
        for copy in chunks[k]:
            copy.wait()
        chunk = lax.rem(me + step, N_CODE)
        for i in range(CHUNK):
            here = pl.ds(i * TILE, TILE)
            window = chunk * CHUNK + i
            total = None
            for j in range(4):
                at = []
                for t in range(2):
                    if j == 1:
                        at.append(ids_ref[window * 2 + t] + blocks)
                        continue
                    number = block_ref[window, me * 2 + t] if j == 0 else listed[(j - 2) * spare + window, me * 2 + t]
                    at.append(jnp.clip(number - me * blocks, 0, blocks - 1))
                part = dg(held[k, j, here, :], pair(factor, at), 1, 0)
                total = part if total is None else total + part
            outs[2 * k + i // 2][pl.ds(i % 2 * TILE, TILE), :] = total


def project(me, block, ids, tiles, r1, r3, factor, pieces, steps):
    smem = pl.BlockSpec(memory_space=SMEM)
    anywhere = pl.BlockSpec(memory_space=pl.ANY)
    n = len(steps)
    spare = r1.shape[0] - tiles.shape[0]
    return pl.pallas_call(
        functools.partial(project_kernel, steps=steps),
        in_specs=[smem, smem, smem, pl.BlockSpec(memory_space=pltpu.HBM)] + [anywhere] * 11,
        out_specs=[pl.BlockSpec(memory_space=VMEM)] * (2 * n),
        out_shape=[jax.ShapeDtypeStruct((CROWS // 2, RANK), F32)] * (2 * n),
        scratch_shapes=[
            pltpu.VMEM((factor.shape[0] + 8 * pieces[0].shape[0], RANK), BF16),
            pltpu.VMEM((n, 4, CROWS, RANK), BF16),
            pltpu.VMEM((2, spare, RANK), BF16),
            pltpu.VMEM((2 * spare, TILE), jnp.int32),
            pltpu.SMEM((2 * spare, TILE), jnp.int32),
            pltpu.SemaphoreType.DMA((12,)),
            pltpu.SemaphoreType.DMA((n, 4)),
        ],
        compiler_params=pltpu.CompilerParams(vmem_limit_bytes=BIG),
        cost_estimate=pl.CostEstimate(flops=n * 10**9, bytes_accessed=(8 + 2 * n) * 10**6, transcendentals=0),
    )(me, block, ids, tiles, r1, r3, factor, *pieces)


def window_kernel(me_ref, counts_ref, *refs):
    parts, (weight_ref, mix_ref, _, _, proj_ref, q_ref, target_ref) = refs[:6], refs[6:]
    me = me_ref[0]
    mix = split(mix_ref[...])
    pids, masks, scaled, factor = [], [], [], []
    for i in range(CHUNK):
        rows = pl.ds(i * TILE, TILE)
        down, along = patients_of(counts_ref, me * CHUNK + i)
        inner = pl.ds(i % 2 * TILE, TILE)
        projected = parts[i // 2][inner, :] + parts[2 + i // 2][inner, :] + parts[4 + i // 2][inner, :]
        proj_ref[rows, :] = projected
        w = [weight_ref[pl.ds(i * 4 + p, 1), :] for p in range(4)]
        row_weight = jnp.where(down == 0, w[0], jnp.where(down == 1, w[1], jnp.where(down == 2, w[2], w[3])))
        pids.append(down)
        masks.append(down == along)
        scaled.append(projected * row_weight)
    scaled_split = [split(s) for s in scaled]
    for i in range(CHUNK):
        mixed = dot3(scaled_split[i], mix, 1, 1)
        squares = jnp.sum(mixed * mixed, axis=1, keepdims=True)
        down = pids[i]
        norm = jnp.zeros_like(squares)
        for p in range(4):
            here = down == p
            total = jnp.sum(jnp.where(here, squares, 0.0), axis=0, keepdims=True)
            norm = jnp.where(here, total, norm)
        factor.append(mixed / jnp.sqrt(norm + EPSILON))
    for _ in range(NS_ITERS):
        halves = [split(f) for f in factor]
        gram = [jnp.where(masks[i], dot3(halves[i], halves[i], 1, 1), 0.0) for i in range(CHUNK)]
        for i in range(CHUNK):
            gh, gl = split(gram[i])
            qh, ql = halves[i]
            moved = dg(jnp.concatenate([gh, gl], axis=1), jnp.concatenate([qh, qh], axis=0), 1, 0) + dg(gh, ql, 1, 0)
            factor[i] = 1.5 * factor[i] - 0.5 * moved
    target = None
    for i in range(CHUNK):
        q_ref[pl.ds(i * TILE, TILE), :] = factor[i]
        part = dot3(factor[i], scaled_split[i], 0, 0)
        target = part if target is None else target + part
    target_ref[...] = target


def window_phase(me, counts, parts, weights, mix, after):
    anywhere = pl.BlockSpec(memory_space=pl.ANY)
    whole = pl.BlockSpec(memory_space=VMEM)
    smem = pl.BlockSpec(memory_space=SMEM)
    block = jax.ShapeDtypeStruct((CROWS, RANK), F32)
    return pl.pallas_call(
        window_kernel,
        in_specs=[smem, smem] + [whole] * 8 + [anywhere] * 2,
        out_specs=[whole] * 3,
        out_shape=[block, block, jax.ShapeDtypeStruct((RANK, RANK), F32)],
        compiler_params=pltpu.CompilerParams(vmem_limit_bytes=40 * 1024 * 1024),
        cost_estimate=pl.CostEstimate(flops=10**9, bytes_accessed=4 * 10**6, transcendentals=0),
    )(me, counts, *parts, weights, mix, *after)


def tail_kernel(me_ref, counts_ref, target_ref, wgram_ref, cgram_ref, mix_ref, q_ref, proj_ref, weight_ref,
                mix_out, weight_out):
    me = me_ref[0]
    target = target_ref[...]
    code_gram = cgram_ref[...]
    curvature = wgram_ref[...] * code_gram
    scale = jnp.sqrt(jnp.sum(curvature * curvature, keepdims=True))
    curved = split(curvature)
    mixing = mix_ref[...]
    for _ in range(NNLS_ITERS):
        mixing = jnp.maximum(mixing - (dot3(mixing, curved) - target) / scale, 0.0)
    mix_out[...] = mixing
    halves = split(mixing)
    second = dot3(halves, halves, 0, 0) * code_gram
    second_scale = jnp.sqrt(jnp.sum(second * second, keepdims=True))
    terms = []
    for i in range(CHUNK):
        rows = pl.ds(i * TILE, TILE)
        down, _ = patients_of(counts_ref, me * CHUNK + i)
        product = proj_ref[rows, :] * dot3(q_ref[rows, :], halves)
        for p in range(4):
            terms.append(jnp.sum(jnp.where(down == p, product, 0.0), axis=0, keepdims=True))
    terms = jnp.concatenate(terms, axis=0)
    seconds = split(second)
    weight = weight_ref[...]
    for _ in range(NNLS_ITERS):
        weight = jnp.maximum(weight - (dot3(weight, seconds) - terms) / second_scale, 0.0)
    weight_out[...] = weight


def place_kernel(me_ref, *refs):
    for s in range(N_CODE):

        @pl.when(pl.program_id(0) == s)
        def _(s=s):
            refs[N_CODE][...] = refs[s][...]


def place(me, parts):
    return pl.pallas_call(
        place_kernel,
        grid_spec=pltpu.PrefetchScalarGridSpec(
            num_scalar_prefetch=1,
            grid=(N_CODE,),
            in_specs=[pl.BlockSpec((CROWS, RANK), lambda g, m: (0, 0))] * N_CODE,
            out_specs=pl.BlockSpec((CROWS, RANK), lambda g, m: (lax.rem(m[0] + N_CODE - g, N_CODE), 0)),
        ),
        out_shape=jax.ShapeDtypeStruct((N_CODE * CROWS, RANK), F32),
        cost_estimate=pl.CostEstimate(flops=0, bytes_accessed=4 * 10**6, transcendentals=0),
    )(me, *parts)


def tail_phase(me, counts, target, wgram, cgram, mix, q, proj, weights):
    whole = pl.BlockSpec(memory_space=VMEM)
    smem = pl.BlockSpec(memory_space=SMEM)
    return pl.pallas_call(
        tail_kernel,
        in_specs=[smem, smem] + [whole] * 7,
        out_specs=[whole, whole],
        out_shape=[
            jax.ShapeDtypeStruct((RANK, RANK), F32),
            jax.ShapeDtypeStruct((CHUNK * 4, RANK), F32),
        ],
        compiler_params=pltpu.CompilerParams(vmem_limit_bytes=40 * 1024 * 1024),
        cost_estimate=pl.CostEstimate(flops=10**9, bytes_accessed=4 * 10**6, transcendentals=0),
    )(me, counts, target, wgram, cgram, mix, q, proj, weights)


def halves_of(x, p):
    half = x.shape[0] // 2
    return lax.dynamic_slice_in_dim(x, p * half, half, 0), lax.dynamic_slice_in_dim(x, (1 - p) * half, half, 0)


def half_sum(x, p):
    kept, passed = halves_of(x, p)
    return kept + shift(passed, "pgroup", 2, 1)


def join(mine, p):
    other = shift(mine, "pgroup", 2, 1)
    return jnp.where(p == 0, jnp.concatenate([mine, other], 0), jnp.concatenate([other, mine], 0))


def around_y(x, step):
    return lax.ppermute(x, "vrow", [(v, v // 4 * 4 + (v + step) % 4) for v in range(32)])


def local(tile_values, tile_block, visit_counts, code_factor, slice_mix, patient_weight):
    c = lax.axis_index("code")
    p = lax.axis_index("pgroup")
    y = lax.axis_index("vrow") % 4
    me = jnp.reshape(c, (1,)).astype(jnp.int32)
    windows = tile_block.shape[0]
    blocks = code_factor.shape[0] // TILE
    piece = code_factor.shape[0] // 8
    first = lax.dynamic_slice_in_dim(code_factor, (y * 2 + p) * piece, piece, 0)
    mine = shift(first, "code", N_CODE, 2)
    up_tiles, down_tiles = pack(me, tile_values, tile_block, first)
    up_tiles, down_tiles, mine = lax.optimization_barrier((up_tiles, down_tiles, mine))
    r1 = shift(up_tiles, "code", N_CODE, 1)
    r3 = shift(down_tiles, "code", N_CODE, 3)
    pieces = [mine] + [around_y(mine, s) for s in (1, 3, 2)]
    pieces = pieces + [shift(x, "pgroup", 2, 1) for x in pieces]

    opposite = (c + 2) % N_CODE
    far_ids = lax.dynamic_slice_in_dim(tile_block, opposite * 2, 2, 1).reshape(-1) - opposite * blocks
    far_ids = jnp.clip(far_ids, 0, blocks - 1)
    per_piece = blocks // 8
    part = far_ids // per_piece
    behind = (y - part // 2) % 4
    behind = jnp.where(behind == 2, 3, jnp.where(behind == 3, 2, behind))
    far_ids = (jnp.where(part % 2 == p, 0, 4) + behind) * per_piece + far_ids % per_piece

    inputs = (me, tile_block, far_ids, tile_values, r1, r3, code_factor, pieces)
    far = project(*inputs, (2,))
    up = shift(far[0], "code", N_CODE, 1)
    down = shift(far[1], "code", N_CODE, 3)
    near = project(*inputs, (1, 3, 0))
    near, up, down = lax.optimization_barrier((near, up, down))
    right, right2, left, left2, kept, kept2 = near
    from_left2 = shift(right2, "code", N_CODE, 1)
    from_right = shift(left, "code", N_CODE, 3)
    from_left = shift(right + up, "code", N_CODE, 1)
    from_right2 = shift(left2 + down, "code", N_CODE, 3)
    parts = (kept, kept2, from_left, from_left2, from_right, from_right2)

    sources, _ = lax.optimization_barrier(([code_factor] + pieces, kept))
    code_part = sum(
        lax.dot_general(x, x, (((0,), (0,)), ((), ())), preferred_element_type=F32) for x in sources
    )
    code_half = halves_of(code_part, p)[0]
    code_gram = join(code_half + shift(code_half, "code", N_CODE, 1), p)
    my_weights = lax.dynamic_slice_in_dim(patient_weight, c * 16, 16, 0)
    weight_part = lax.dot_general(my_weights, my_weights, (((0,), (0,)), ((), ())), precision=lax.Precision.HIGHEST)

    proj, q, target_part = window_phase(me, visit_counts, parts, my_weights, slice_mix, (weight_part, code_gram))
    gathered = [shift(q, "code", N_CODE, s) for s in (1, 3)]
    axes = ("code", "vrow")
    sent = half_sum(jnp.concatenate([target_part, weight_part], axis=1), p)[:, None, :]
    row = jnp.sum(lax.all_to_all(sent, axes, 0, 0, tiled=True), axis=0)
    row, gathered = lax.optimization_barrier((row, gathered))
    last = shift(q, "code", N_CODE, 2)
    spread = jnp.broadcast_to(row[None], (RANK // 2,) + row.shape)
    sums = join(lax.all_to_all(spread, axes, 0, 0, tiled=True)[:, 0, :], p)
    sums, last = lax.optimization_barrier((sums, last))
    gathered = [gathered[0], last, gathered[1]]
    mixing, weight = tail_phase(
        me, visit_counts, sums[:, :RANK], sums[:, RANK:], code_gram, slice_mix, q, proj, my_weights
    )
    factor = place(me, [q] + gathered)
    spread = jnp.broadcast_to(weight[None], (N_CODE,) + weight.shape)
    weight_new = lax.all_to_all(spread, "code", 0, 0, tiled=True).reshape(patient_weight.shape)
    return (factor, mixing, weight_new)


def solution(mesh):
    placed = (
        P(("pgroup", "vrow"), "code"),
        P(("pgroup", "vrow"), "code"),
        P(("pgroup", "vrow"), None),
        P("code", None),
        P(),
        P(("pgroup", "vrow"), None),
    )
    return jax.shard_map(
        local,
        mesh=mesh,
        in_specs=placed,
        out_specs=(P(("pgroup", "vrow"), None), P(), P(("pgroup", "vrow"), None)),
        check_vma=False,
    )
```

```python
import functools

import jax
import jax.numpy as jnp
from jax import lax
from jax.experimental import pallas as pl
from jax.experimental.pallas import tpu as pltpu
from jax.sharding import PartitionSpec as P

TILE = 128
RANK = 256
NS_ITERS = 5
NNLS_ITERS = 4
N_CODE = 4
CHUNK = 4
CROWS = CHUNK * TILE
EPSILON = 1e-06
F32 = jnp.float32
BF16 = jnp.bfloat16
SMEM = pltpu.SMEM
VMEM = pltpu.VMEM
SCOPED = 24 * 1024 * 1024
BIG = 60 * 1024 * 1024


def shift(x, axis, n, step):
    return lax.ppermute(x, axis, [(i, (i + step) % n) for i in range(n)])


def dg(a, b, ca, cb):
    return lax.dot_general(a, b, (((ca,), (cb,)), ((), ())), preferred_element_type=F32)


def split(a):
    high = a.astype(BF16)
    return high, (a - high.astype(F32)).astype(BF16)


def dot3(a, b, ca=1, cb=0):
    ah, al = a if isinstance(a, tuple) else split(a)
    bh, bl = b if isinstance(b, tuple) else split(b)
    return dg(ah, bh, ca, cb) + (dg(ah, bl, ca, cb) + dg(al, bh, ca, cb))


def patients_of(counts_ref, window):
    e0 = counts_ref[window, 0]
    e1 = e0 + counts_ref[window, 1]
    e2 = e1 + counts_ref[window, 2]
    down = lax.broadcasted_iota(jnp.int32, (TILE, 1), 0)
    along = lax.broadcasted_iota(jnp.int32, (1, TILE), 1)

    def number(i):
        return (i >= e0).astype(jnp.int32) + (i >= e1).astype(jnp.int32) + (i >= e2).astype(jnp.int32)

    return number(down), number(along)


def pack_kernel(me_ref, tiles_ref, block_ref, first_ref, up_ref, down_ref, held, sems):
    rows, spare = tiles_ref.shape[0], block_ref.shape[0]
    half = rows // 2
    fetch = []
    for k, step in enumerate((1, 3)):
        at = pl.multiple_of(lax.rem(me_ref[0] + step, N_CODE) * RANK, RANK)
        for j in range(2):
            here = pl.ds(j * half, half)
            fetch.append(pltpu.make_async_copy(tiles_ref.at[here, pl.ds(at, RANK)], held.at[k, here, :], sems.at[k, j]))
    for copy in fetch:
        copy.start()
    width = block_ref.shape[1]
    place = lax.broadcasted_iota(jnp.int32, (width, RANK), 0) == lax.broadcasted_iota(jnp.int32, (width, RANK), 1)
    numbers = dg(block_ref[...].astype(F32).astype(BF16), jnp.where(place, 1.0, 0.0).astype(BF16), 1, 0).astype(BF16)
    send = []
    for k, ref in enumerate((up_ref, down_ref)):
        held[k, pl.ds(rows, spare), :] = numbers
        for j, size in enumerate((half, half + spare)):
            here = pl.ds(j * half, size)
            send.append(pltpu.make_async_copy(held.at[k, here, :], ref.at[here, :], sems.at[k, 2 + j]))
    for arrived, copy in zip(fetch, send):
        arrived.wait()
        copy.start()
    for copy in send:
        copy.wait()


def pack(me, tiles, block, first):
    whole = pl.BlockSpec(memory_space=VMEM)
    rows = tiles.shape[0] + block.shape[0]
    return pl.pallas_call(
        pack_kernel,
        in_specs=[pl.BlockSpec(memory_space=SMEM), pl.BlockSpec(memory_space=pltpu.HBM), whole, pl.BlockSpec(memory_space=pl.ANY)],
        out_specs=[pl.BlockSpec(memory_space=pl.ANY)] * 2,
        out_shape=[jax.ShapeDtypeStruct((rows, RANK), BF16)] * 2,
        scratch_shapes=[pltpu.VMEM((2, rows, RANK), BF16), pltpu.SemaphoreType.DMA((2, 4))],
        compiler_params=pltpu.CompilerParams(vmem_limit_bytes=BIG),
        cost_estimate=pl.CostEstimate(flops=0, bytes_accessed=4 * 10**6, transcendentals=0),
    )(me, tiles, block, first)


def gram_kernel(factor_ref, after_ref, gram_ref, factor, sem):
    table = pltpu.make_async_copy(factor_ref, factor, sem)
    table.start()
    table.wait()
    part = 512
    gram_ref[...] = jnp.zeros_like(gram_ref)

    def one(k, carry):
        rows = factor[pl.ds(pl.multiple_of(k * part, part), part), :]
        gram_ref[...] += dg(rows, rows, 0, 0)
        return carry

    lax.fori_loop(0, factor.shape[0] // part, one, 0)


def gram(factor, after):
    return pl.pallas_call(
        gram_kernel,
        in_specs=[pl.BlockSpec(memory_space=pltpu.HBM), pl.BlockSpec(memory_space=pl.ANY)],
        out_specs=pl.BlockSpec(memory_space=VMEM),
        out_shape=jax.ShapeDtypeStruct((RANK, RANK), F32),
        scratch_shapes=[pltpu.VMEM(factor.shape, BF16), pltpu.SemaphoreType.DMA],
        compiler_params=pltpu.CompilerParams(vmem_limit_bytes=63 * 1024 * 1024),
        cost_estimate=pl.CostEstimate(flops=10**9, bytes_accessed=7 * 10**6, transcendentals=0),
    )(factor, after)


def pair(factor_ref, at):
    return jnp.concatenate([factor_ref[pl.ds(pl.multiple_of(x * TILE, TILE), TILE), :] for x in at], axis=0)


def count_outputs(steps):
    return sum(1 if step == 0 else 2 for step in steps)


def project_kernel(me_ref, block_ref, ids_ref, tiles_ref, r1_ref, r3_ref, factor_ref, *refs, steps):
    n = len(steps)
    pieces, outs = refs[:8], refs[8 : 8 + count_outputs(steps)]
    factor, held, raw, wide, listed, sems, chunk_sems = refs[8 + count_outputs(steps) :]
    me = me_ref[0]
    rows = tiles_ref.shape[0]
    spare = r1_ref.shape[0] - rows
    local_rows = factor_ref.shape[0]
    blocks = local_rows // TILE
    piece = pieces[0].shape[0]
    numbers = [pltpu.make_async_copy(r.at[pl.ds(rows, spare), :], raw.at[k], sems.at[k]) for k, r in enumerate((r1_ref, r3_ref))]
    tables = [pltpu.make_async_copy(factor_ref, factor.at[pl.ds(0, local_rows), :], sems.at[2])]
    for k, ref in enumerate(pieces):
        tables.append(pltpu.make_async_copy(ref, factor.at[pl.ds(local_rows + k * piece, piece), :], sems.at[3 + k]))
    chunks = []
    for k, step in enumerate(steps):
        here = pl.ds(pl.multiple_of(lax.rem(me + step, N_CODE) * CROWS, CROWS), CROWS)
        sources = [tiles_ref.at[here, pl.ds(pl.multiple_of(x * RANK, RANK), RANK)] for x in (me, lax.rem(me + 2, N_CODE))]
        sources += [r1_ref.at[here, :], r3_ref.at[here, :]]
        chunks.append([pltpu.make_async_copy(x, held.at[k, j], chunk_sems.at[k, j]) for j, x in enumerate(sources)])
    for copy in numbers + tables[:1] + sum(chunks, []) + tables[1:]:
        copy.start()
    for copy in numbers:
        copy.wait()
    for k in range(2):
        wide[pl.ds(k * spare, spare), :] = raw[k, :, 0:TILE].astype(F32).astype(jnp.int32)
    down = pltpu.make_async_copy(wide, listed, sems.at[11])
    down.start()
    tables[0].wait()
    down.wait()

    def product(k, i, window, j):
        at = []
        for t in range(2):
            if j == 1:
                at.append(ids_ref[window * 2 + t] + blocks)
                continue
            number = block_ref[window, me * 2 + t] if j == 0 else listed[(j - 2) * spare + window, me * 2 + t]
            at.append(jnp.clip(number - me * blocks, 0, blocks - 1))
        return dg(held[k, j, pl.ds(i * TILE, TILE), :], pair(factor, at), 1, 0)

    for late in (False, True):
        for copy in tables[1:] if late else []:
            copy.wait()
        for k, step in enumerate(steps):
            for copy in [] if late else chunks[k]:
                copy.wait()
            for i in range(CHUNK):
                window = lax.rem(me + step, N_CODE) * CHUNK + i
                out, here = outs[2 * k if step == 0 else 2 * k + i // 2], pl.ds((i if step == 0 else i % 2) * TILE, TILE)
                if late:
                    out[here, :] += product(k, i, window, 1)
                else:
                    out[here, :] = product(k, i, window, 0) + product(k, i, window, 2) + product(k, i, window, 3)


def project(me, block, ids, tiles, r1, r3, factor, pieces, steps):
    smem = pl.BlockSpec(memory_space=SMEM)
    anywhere = pl.BlockSpec(memory_space=pl.ANY)
    hbm = pl.BlockSpec(memory_space=pltpu.HBM)
    n = len(steps)
    spare = r1.shape[0] - tiles.shape[0]
    return pl.pallas_call(
        functools.partial(project_kernel, steps=steps),
        in_specs=[smem, smem, smem, hbm, anywhere, anywhere, hbm] + [anywhere] * 8,
        out_specs=[pl.BlockSpec(memory_space=VMEM)] * count_outputs(steps),
        out_shape=[
            jax.ShapeDtypeStruct((size, RANK), F32) for step in steps for size in ([CROWS] if step == 0 else [CROWS // 2] * 2)
        ],
        scratch_shapes=[
            pltpu.VMEM((factor.shape[0] + 8 * pieces[0].shape[0], RANK), BF16),
            pltpu.VMEM((n, 4, CROWS, RANK), BF16),
            pltpu.VMEM((2, spare, RANK), BF16),
            pltpu.VMEM((2 * spare, TILE), jnp.int32),
            pltpu.SMEM((2 * spare, TILE), jnp.int32),
            pltpu.SemaphoreType.DMA((12,)),
            pltpu.SemaphoreType.DMA((n, 4)),
        ],
        compiler_params=pltpu.CompilerParams(vmem_limit_bytes=BIG),
        cost_estimate=pl.CostEstimate(flops=n * 10**9, bytes_accessed=(8 + 2 * n) * 10**6, transcendentals=0),
    )(me, block, ids, tiles, r1, r3, factor, *pieces)


def window_kernel(me_ref, core_ref, counts_ref, weight_ref, *refs):
    parts, (mix_ref, proj_ref, q_ref, kept_ref, passed_ref) = refs[:5], refs[5:]
    me = me_ref[0]
    weights = split(weight_ref[...])
    weight_gram = dot3(weights, weights, 0, 0)
    mix = split(mix_ref[...])
    pids, masks, scaled, factor = [], [], [], []
    for i in range(CHUNK):
        rows = pl.ds(i * TILE, TILE)
        down, along = patients_of(counts_ref, me * CHUNK + i)
        inner = pl.ds(i % 2 * TILE, TILE)
        projected = parts[0][rows, :] + parts[1 + i // 2][inner, :] + parts[3 + i // 2][inner, :]
        proj_ref[rows, :] = projected
        w = [weight_ref[pl.ds(i * 4 + p, 1), :] for p in range(4)]
        row_weight = jnp.where(down == 0, w[0], jnp.where(down == 1, w[1], jnp.where(down == 2, w[2], w[3])))
        pids.append(down)
        masks.append(down == along)
        scaled.append(projected * row_weight)
    scaled_split = [split(s) for s in scaled]
    for i in range(CHUNK):
        mixed = dot3(scaled_split[i], mix, 1, 1)
        squares = jnp.sum(mixed * mixed, axis=1, keepdims=True)
        down = pids[i]
        norm = jnp.zeros_like(squares)
        for p in range(4):
            here = down == p
            total = jnp.sum(jnp.where(here, squares, 0.0), axis=0, keepdims=True)
            norm = jnp.where(here, total, norm)
        factor.append(mixed / jnp.sqrt(norm + EPSILON))
    for _ in range(NS_ITERS):
        halves = [split(f) for f in factor]
        gram = [jnp.where(masks[i], dot3(halves[i], halves[i], 1, 1), 0.0) for i in range(CHUNK)]
        for i in range(CHUNK):
            gh, gl = split(gram[i])
            qh, ql = halves[i]
            moved = dg(jnp.concatenate([gh, gl], axis=1), jnp.concatenate([qh, qh], axis=0), 1, 0) + dg(gh, ql, 1, 0)
            factor[i] = 1.5 * factor[i] - 0.5 * moved
    target = None
    for i in range(CHUNK):
        q_ref[pl.ds(i * TILE, TILE), :] = factor[i]
        part = dot3(factor[i], scaled_split[i], 0, 0)
        target = part if target is None else target + part
    half = RANK // 2
    for ref, first in ((kept_ref, core_ref[0] == 0), (passed_ref, core_ref[0] != 0)):
        ref[:, 0:RANK] = jnp.where(first, target[:half], target[half:])
        ref[:, RANK : 2 * RANK] = jnp.where(first, weight_gram[:half], weight_gram[half:])


def window_phase(me, core, counts, weights, parts, mix):
    whole = pl.BlockSpec(memory_space=VMEM)
    smem = pl.BlockSpec(memory_space=SMEM)
    block = jax.ShapeDtypeStruct((CROWS, RANK), F32)
    half = jax.ShapeDtypeStruct((RANK // 2, 2 * RANK), F32)
    return pl.pallas_call(
        window_kernel,
        in_specs=[smem, smem, smem] + [whole] * 7,
        out_specs=[whole] * 4,
        out_shape=[block, block, half, half],
        compiler_params=pltpu.CompilerParams(vmem_limit_bytes=40 * 1024 * 1024),
        cost_estimate=pl.CostEstimate(flops=10**9, bytes_accessed=4 * 10**6, transcendentals=0),
    )(me, core, counts, weights, *parts, mix)


def tail_kernel(me_ref, counts_ref, sums_ref, cgram_ref, mix_ref, q_ref, proj_ref, weight_ref,
                mix_out, weight_out):
    me = me_ref[0]
    target = sums_ref[:, 0:RANK]
    code_gram = cgram_ref[...]
    curvature = sums_ref[:, RANK : 2 * RANK] * code_gram
    scale = jnp.sqrt(jnp.sum(curvature * curvature, keepdims=True))
    curved = split(curvature)
    mixing = mix_ref[...]
    for _ in range(NNLS_ITERS):
        mixing = jnp.maximum(mixing - (dot3(mixing, curved) - target) / scale, 0.0)
    mix_out[...] = mixing
    halves = split(mixing)
    second = dot3(halves, halves, 0, 0) * code_gram
    second_scale = jnp.sqrt(jnp.sum(second * second, keepdims=True))
    terms = []
    for i in range(CHUNK):
        rows = pl.ds(i * TILE, TILE)
        down, _ = patients_of(counts_ref, me * CHUNK + i)
        product = proj_ref[rows, :] * dot3(q_ref[rows, :], halves)
        for p in range(4):
            terms.append(jnp.sum(jnp.where(down == p, product, 0.0), axis=0, keepdims=True))
    terms = jnp.concatenate(terms, axis=0)
    seconds = split(second)
    weight = weight_ref[...]
    for _ in range(NNLS_ITERS):
        weight = jnp.maximum(weight - (dot3(weight, seconds) - terms) / second_scale, 0.0)
    for s in range(N_CODE):
        weight_out[s] = weight


def place_kernel(me_ref, q_ref, left_ref, right_ref, first_ref, second_ref, out_ref):
    half = CROWS // 2

    def put(step, rows, ref):
        @pl.when(pl.program_id(0) == step)
        def _():
            out_ref[rows, :] = ref[...]

    everything = pl.ds(0, CROWS)
    put(0, everything, q_ref)
    put(1, everything, left_ref)
    put(2, pl.ds(0, half), first_ref)
    put(2, pl.ds(half, half), second_ref)
    put(3, everything, right_ref)


def place(me, parts):
    return pl.pallas_call(
        place_kernel,
        grid_spec=pltpu.PrefetchScalarGridSpec(
            num_scalar_prefetch=1,
            grid=(N_CODE,),
            in_specs=[pl.BlockSpec(x.shape, lambda g, m: (0, 0)) for x in parts],
            out_specs=pl.BlockSpec((CROWS, RANK), lambda g, m: (lax.rem(m[0] + N_CODE - g, N_CODE), 0)),
        ),
        out_shape=jax.ShapeDtypeStruct((N_CODE * CROWS, RANK), F32),
        cost_estimate=pl.CostEstimate(flops=0, bytes_accessed=4 * 10**6, transcendentals=0),
    )(me, *parts)


def tail_phase(me, counts, sums, cgram, mix, q, proj, weights):
    whole = pl.BlockSpec(memory_space=VMEM)
    smem = pl.BlockSpec(memory_space=SMEM)
    return pl.pallas_call(
        tail_kernel,
        in_specs=[smem, smem] + [whole] * 6,
        out_specs=[whole, whole],
        out_shape=[
            jax.ShapeDtypeStruct((RANK, RANK), F32),
            jax.ShapeDtypeStruct((N_CODE, CHUNK * 4, RANK), F32),
        ],
        compiler_params=pltpu.CompilerParams(vmem_limit_bytes=SCOPED),
        cost_estimate=pl.CostEstimate(flops=10**9, bytes_accessed=4 * 10**6, transcendentals=0),
    )(me, counts, sums, cgram, mix, q, proj, weights)


def halves_of(x, p):
    half = x.shape[0] // 2
    return lax.dynamic_slice_in_dim(x, p * half, half, 0), lax.dynamic_slice_in_dim(x, (1 - p) * half, half, 0)


def join(mine, p):
    other = shift(mine, "pgroup", 2, 1)
    return jnp.where(p == 0, jnp.concatenate([mine, other], 0), jnp.concatenate([other, mine], 0))


def around_y(x, step):
    return lax.ppermute(x, "vrow", [(v, v // 4 * 4 + (v + step) % 4) for v in range(32)])


def local(tile_values, tile_block, visit_counts, code_factor, slice_mix, patient_weight):
    c = lax.axis_index("code")
    p = lax.axis_index("pgroup")
    y = lax.axis_index("vrow") % 4
    me = jnp.reshape(c, (1,)).astype(jnp.int32)
    windows = tile_block.shape[0]
    blocks = code_factor.shape[0] // TILE
    piece = code_factor.shape[0] // 8
    first = lax.dynamic_slice_in_dim(code_factor, (y * 2 + p) * piece, piece, 0)
    mine = shift(first, "code", N_CODE, 2)
    up_tiles, down_tiles = pack(me, tile_values, tile_block, first)
    up_tiles, down_tiles, mine = lax.optimization_barrier((up_tiles, down_tiles, mine))
    r1 = shift(up_tiles, "code", N_CODE, 1)
    r3 = shift(down_tiles, "code", N_CODE, 3)
    pieces = [mine] + [around_y(mine, s) for s in (1, 3, 2)]
    code_part = gram(code_factor, first)
    pieces, code_part = lax.optimization_barrier((pieces, code_part))
    pieces = pieces + [shift(x, "pgroup", 2, 1) for x in pieces]

    opposite = (c + 2) % N_CODE
    far_ids = lax.dynamic_slice_in_dim(tile_block, opposite * 2, 2, 1).reshape(-1) - opposite * blocks
    far_ids = jnp.clip(far_ids, 0, blocks - 1)
    per_piece = blocks // 8
    part = far_ids // per_piece
    behind = (y - part // 2) % 4
    behind = jnp.where(behind == 2, 3, jnp.where(behind == 3, 2, behind))
    far_ids = (jnp.where(part % 2 == p, 0, 4) + behind) * per_piece + far_ids % per_piece

    inputs = (me, tile_block, far_ids, tile_values, r1, r3, code_factor, pieces)
    far = project(*inputs, (2,))
    up = shift(far[0], "code", N_CODE, 1)
    down = shift(far[1], "code", N_CODE, 3)
    near = project(*inputs, (1, 3, 0))
    near, up, down = lax.optimization_barrier((near, up, down))
    right, right2, left, left2, kept = near
    from_left2 = shift(right2, "code", N_CODE, 1)
    from_right = shift(left, "code", N_CODE, 3)
    from_left = shift(right + up, "code", N_CODE, 1)
    from_right2 = shift(left2 + down, "code", N_CODE, 3)
    parts = (kept, from_left, from_left2, from_right, from_right2)

    my_weights = lax.dynamic_slice_in_dim(patient_weight, c * 16, 16, 0)
    core = jnp.reshape(p, (1,)).astype(jnp.int32)
    code_half = halves_of(code_part, p)[0]
    code_half = code_half + shift(code_half, "code", N_CODE, 2)
    parts, code_half = lax.optimization_barrier((parts, code_half))
    proj, q, sent, passed = window_phase(me, core, visit_counts, my_weights, parts, slice_mix)
    axes = ("code", "vrow")
    gathered = [shift(q, "code", N_CODE, s) for s in (1, 3)]
    sent = (sent + shift(passed, "pgroup", 2, 1))[:, None, :]
    row = jnp.sum(lax.all_to_all(sent, axes, 0, 0, tiled=True), axis=0)
    code_half = code_half + shift(code_half, "code", N_CODE, 1)
    row, gathered, code_half = lax.optimization_barrier((row, gathered, code_half))
    code_gram = join(code_half, p)
    half = CROWS // 2
    last = [shift(gathered[0][:half], "code", N_CODE, 1), shift(gathered[1][half:], "code", N_CODE, 3)]
    spread = jnp.broadcast_to(row[None], (RANK // 2,) + row.shape)
    back, last = lax.optimization_barrier((lax.all_to_all(spread, axes, 0, 0, tiled=True), last))
    sums = join(back[:, 0, :], p)
    mixing, spread = tail_phase(me, visit_counts, sums, code_gram, slice_mix, q, proj, my_weights)
    factor = place(me, [q, gathered[0], gathered[1]] + last)
    weight_new = lax.all_to_all(spread, "code", 0, 0, tiled=True).reshape(patient_weight.shape)
    return (factor, mixing, weight_new)


def solution(mesh):
    placed = (
        P(("pgroup", "vrow"), "code"),
        P(("pgroup", "vrow"), "code"),
        P(("pgroup", "vrow"), None),
        P("code", None),
        P(),
        P(("pgroup", "vrow"), None),
    )
    return jax.shard_map(
        local,
        mesh=mesh,
        in_specs=placed,
        out_specs=(P(("pgroup", "vrow"), None), P(), P(("pgroup", "vrow"), None)),
        check_vma=False,
    )
```

```python
import functools

import jax
import jax.numpy as jnp
from jax import lax
from jax.experimental import pallas as pl
from jax.experimental.pallas import tpu as pltpu
from jax.sharding import PartitionSpec as P

TILE = 128
RANK = 256
NS_ITERS = 5
NNLS_ITERS = 4
N_CODE = 4
CHUNK = 4
CROWS = CHUNK * TILE
EPSILON = 1e-06
F32 = jnp.float32
BF16 = jnp.bfloat16
SMEM = pltpu.SMEM
VMEM = pltpu.VMEM
SCOPED = 24 * 1024 * 1024
BIG = 60 * 1024 * 1024


def shift(x, axis, n, step):
    return lax.ppermute(x, axis, [(i, (i + step) % n) for i in range(n)])


def dg(a, b, ca, cb):
    return lax.dot_general(a, b, (((ca,), (cb,)), ((), ())), preferred_element_type=F32)


def split(a):
    high = a.astype(BF16)
    return high, (a - high.astype(F32)).astype(BF16)


def dot3(a, b, ca=1, cb=0):
    ah, al = a if isinstance(a, tuple) else split(a)
    bh, bl = b if isinstance(b, tuple) else split(b)
    return dg(ah, bh, ca, cb) + (dg(ah, bl, ca, cb) + dg(al, bh, ca, cb))


def patients_of(counts_ref, window):
    e0 = counts_ref[window, 0]
    e1 = e0 + counts_ref[window, 1]
    e2 = e1 + counts_ref[window, 2]
    down = lax.broadcasted_iota(jnp.int32, (TILE, 1), 0)
    along = lax.broadcasted_iota(jnp.int32, (1, TILE), 1)

    def number(i):
        return (i >= e0).astype(jnp.int32) + (i >= e1).astype(jnp.int32) + (i >= e2).astype(jnp.int32)

    return number(down), number(along)


def pack_kernel(me_ref, tiles_ref, block_ref, first_ref, up_ref, down_ref, held, sems):
    rows, spare = tiles_ref.shape[0], block_ref.shape[0]
    half = rows // 2
    fetch = []
    for k, step in enumerate((1, 3)):
        at = pl.multiple_of(lax.rem(me_ref[0] + step, N_CODE) * RANK, RANK)
        for j in range(2):
            here = pl.ds(j * half, half)
            fetch.append(pltpu.make_async_copy(tiles_ref.at[here, pl.ds(at, RANK)], held.at[k, here, :], sems.at[k, j]))
    for copy in fetch:
        copy.start()
    width = block_ref.shape[1]
    place = lax.broadcasted_iota(jnp.int32, (width, RANK), 0) == lax.broadcasted_iota(jnp.int32, (width, RANK), 1)
    numbers = dg(block_ref[...].astype(F32).astype(BF16), jnp.where(place, 1.0, 0.0).astype(BF16), 1, 0).astype(BF16)
    send = []
    for k, ref in enumerate((up_ref, down_ref)):
        held[k, pl.ds(rows, spare), :] = numbers
        for j, size in enumerate((half, half + spare)):
            here = pl.ds(j * half, size)
            send.append(pltpu.make_async_copy(held.at[k, here, :], ref.at[here, :], sems.at[k, 2 + j]))
    for arrived, copy in zip(fetch, send):
        arrived.wait()
        copy.start()
    for copy in send:
        copy.wait()


def pack(me, tiles, block, first):
    whole = pl.BlockSpec(memory_space=VMEM)
    rows = tiles.shape[0] + block.shape[0]
    return pl.pallas_call(
        pack_kernel,
        in_specs=[pl.BlockSpec(memory_space=SMEM), pl.BlockSpec(memory_space=pltpu.HBM), whole, pl.BlockSpec(memory_space=pl.ANY)],
        out_specs=[pl.BlockSpec(memory_space=pl.ANY)] * 2,
        out_shape=[jax.ShapeDtypeStruct((rows, RANK), BF16)] * 2,
        scratch_shapes=[pltpu.VMEM((2, rows, RANK), BF16), pltpu.SemaphoreType.DMA((2, 4))],
        compiler_params=pltpu.CompilerParams(vmem_limit_bytes=BIG),
        cost_estimate=pl.CostEstimate(flops=0, bytes_accessed=4 * 10**6, transcendentals=0),
    )(me, tiles, block, first)


def gram_kernel(factor_ref, after_ref, gram_ref, factor, sem):
    table = pltpu.make_async_copy(factor_ref, factor, sem)
    table.start()
    table.wait()
    part = 512
    gram_ref[...] = jnp.zeros_like(gram_ref)

    def one(k, carry):
        rows = factor[pl.ds(pl.multiple_of(k * part, part), part), :]
        gram_ref[...] += dg(rows, rows, 0, 0)
        return carry

    lax.fori_loop(0, factor.shape[0] // part, one, 0)


def gram(factor, after):
    return pl.pallas_call(
        gram_kernel,
        in_specs=[pl.BlockSpec(memory_space=pltpu.HBM), pl.BlockSpec(memory_space=pl.ANY)],
        out_specs=pl.BlockSpec(memory_space=VMEM),
        out_shape=jax.ShapeDtypeStruct((RANK, RANK), F32),
        scratch_shapes=[pltpu.VMEM(factor.shape, BF16), pltpu.SemaphoreType.DMA],
        compiler_params=pltpu.CompilerParams(vmem_limit_bytes=63 * 1024 * 1024),
        cost_estimate=pl.CostEstimate(flops=10**9, bytes_accessed=7 * 10**6, transcendentals=0),
    )(factor, after)


def pair(factor_ref, at):
    return jnp.concatenate([factor_ref[pl.ds(pl.multiple_of(x * TILE, TILE), TILE), :] for x in at], axis=0)


def count_outputs(steps):
    return sum(1 if step == 0 else 2 for step in steps)


def project_kernel(me_ref, block_ref, ids_ref, tiles_ref, r1_ref, r3_ref, factor_ref, *refs, steps):
    n = len(steps)
    pieces, outs = refs[:8], refs[8 : 8 + count_outputs(steps)]
    factor, held, raw, wide, listed, sems, chunk_sems = refs[8 + count_outputs(steps) :]
    me = me_ref[0]
    rows = tiles_ref.shape[0]
    spare = r1_ref.shape[0] - rows
    local_rows = factor_ref.shape[0]
    blocks = local_rows // TILE
    piece = pieces[0].shape[0]
    numbers = [pltpu.make_async_copy(r.at[pl.ds(rows, spare), :], raw.at[k], sems.at[k]) for k, r in enumerate((r1_ref, r3_ref))]
    tables = [pltpu.make_async_copy(factor_ref, factor.at[pl.ds(0, local_rows), :], sems.at[2])]
    for k, ref in enumerate(pieces):
        tables.append(pltpu.make_async_copy(ref, factor.at[pl.ds(local_rows + k * piece, piece), :], sems.at[3 + k]))
    chunks = []
    for k, step in enumerate(steps):
        here = pl.ds(pl.multiple_of(lax.rem(me + step, N_CODE) * CROWS, CROWS), CROWS)
        sources = [tiles_ref.at[here, pl.ds(pl.multiple_of(x * RANK, RANK), RANK)] for x in (me, lax.rem(me + 2, N_CODE))]
        sources += [r1_ref.at[here, :], r3_ref.at[here, :]]
        chunks.append([pltpu.make_async_copy(x, held.at[k, j], chunk_sems.at[k, j]) for j, x in enumerate(sources)])
    for copy in numbers + tables[:1] + sum(chunks, []) + tables[1:]:
        copy.start()
    for copy in numbers:
        copy.wait()
    for k in range(2):
        wide[pl.ds(k * spare, spare), :] = raw[k, :, 0:TILE].astype(F32).astype(jnp.int32)
    down = pltpu.make_async_copy(wide, listed, sems.at[11])
    down.start()
    tables[0].wait()
    down.wait()

    def product(k, i, window, j):
        at = []
        for t in range(2):
            if j == 1:
                at.append(ids_ref[window * 2 + t] + blocks)
                continue
            number = block_ref[window, me * 2 + t] if j == 0 else listed[(j - 2) * spare + window, me * 2 + t]
            at.append(jnp.clip(number - me * blocks, 0, blocks - 1))
        return dg(held[k, j, pl.ds(i * TILE, TILE), :], pair(factor, at), 1, 0)

    for late in (False, True):
        for copy in tables[1:] if late else []:
            copy.wait()
        for k, step in enumerate(steps):
            for copy in [] if late else chunks[k]:
                copy.wait()
            for i in range(CHUNK):
                window = lax.rem(me + step, N_CODE) * CHUNK + i
                out, here = outs[2 * k if step == 0 else 2 * k + i // 2], pl.ds((i if step == 0 else i % 2) * TILE, TILE)
                if late:
                    out[here, :] += product(k, i, window, 1)
                else:
                    out[here, :] = product(k, i, window, 0) + product(k, i, window, 2) + product(k, i, window, 3)


def project(me, block, ids, tiles, r1, r3, factor, pieces, steps):
    smem = pl.BlockSpec(memory_space=SMEM)
    anywhere = pl.BlockSpec(memory_space=pl.ANY)
    hbm = pl.BlockSpec(memory_space=pltpu.HBM)
    n = len(steps)
    spare = r1.shape[0] - tiles.shape[0]
    return pl.pallas_call(
        functools.partial(project_kernel, steps=steps),
        in_specs=[smem, smem, smem, hbm, anywhere, anywhere, hbm] + [anywhere] * 8,
        out_specs=[pl.BlockSpec(memory_space=VMEM)] * count_outputs(steps),
        out_shape=[
            jax.ShapeDtypeStruct((size, RANK), F32) for step in steps for size in ([CROWS] if step == 0 else [CROWS // 2] * 2)
        ],
        scratch_shapes=[
            pltpu.VMEM((factor.shape[0] + 8 * pieces[0].shape[0], RANK), BF16),
            pltpu.VMEM((n, 4, CROWS, RANK), BF16),
            pltpu.VMEM((2, spare, RANK), BF16),
            pltpu.VMEM((2 * spare, TILE), jnp.int32),
            pltpu.SMEM((2 * spare, TILE), jnp.int32),
            pltpu.SemaphoreType.DMA((12,)),
            pltpu.SemaphoreType.DMA((n, 4)),
        ],
        compiler_params=pltpu.CompilerParams(vmem_limit_bytes=BIG),
        cost_estimate=pl.CostEstimate(flops=n * 10**9, bytes_accessed=(8 + 2 * n) * 10**6, transcendentals=0),
    )(me, block, ids, tiles, r1, r3, factor, *pieces)


def window_kernel(me_ref, core_ref, counts_ref, weight_ref, *refs):
    parts, (mix_ref, proj_ref, q_ref, kept_ref, passed_ref) = refs[:5], refs[5:]
    me = me_ref[0]
    weights = split(weight_ref[...])
    weight_gram = dot3(weights, weights, 0, 0)
    mix = split(mix_ref[...])
    pids, masks, scaled, factor = [], [], [], []
    for i in range(CHUNK):
        rows = pl.ds(i * TILE, TILE)
        down, along = patients_of(counts_ref, me * CHUNK + i)
        inner = pl.ds(i % 2 * TILE, TILE)
        projected = parts[0][rows, :] + parts[1 + i // 2][inner, :] + parts[3 + i // 2][inner, :]
        proj_ref[rows, :] = projected
        w = [weight_ref[pl.ds(i * 4 + p, 1), :] for p in range(4)]
        row_weight = jnp.where(down == 0, w[0], jnp.where(down == 1, w[1], jnp.where(down == 2, w[2], w[3])))
        pids.append(down)
        masks.append(down == along)
        scaled.append(projected * row_weight)
    scaled_split = [split(s) for s in scaled]
    for i in range(CHUNK):
        mixed = dot3(scaled_split[i], mix, 1, 1)
        squares = jnp.sum(mixed * mixed, axis=1, keepdims=True)
        down = pids[i]
        norm = jnp.zeros_like(squares)
        for p in range(4):
            here = down == p
            total = jnp.sum(jnp.where(here, squares, 0.0), axis=0, keepdims=True)
            norm = jnp.where(here, total, norm)
        factor.append(mixed / jnp.sqrt(norm + EPSILON))
    for _ in range(NS_ITERS):
        halves = [split(f) for f in factor]
        gram = [jnp.where(masks[i], dot3(halves[i], halves[i], 1, 1), 0.0) for i in range(CHUNK)]
        for i in range(CHUNK):
            gh, gl = split(gram[i])
            qh, ql = halves[i]
            moved = dg(jnp.concatenate([gh, gl], axis=1), jnp.concatenate([qh, qh], axis=0), 1, 0) + dg(gh, ql, 1, 0)
            factor[i] = 1.5 * factor[i] - 0.5 * moved
    target = None
    for i in range(CHUNK):
        q_ref[pl.ds(i * TILE, TILE), :] = factor[i]
        part = dot3(factor[i], scaled_split[i], 0, 0)
        target = part if target is None else target + part
    half = RANK // 2
    for ref, first in ((kept_ref, core_ref[0] == 0), (passed_ref, core_ref[0] != 0)):
        ref[:, 0:RANK] = jnp.where(first, target[:half], target[half:])
        ref[:, RANK : 2 * RANK] = jnp.where(first, weight_gram[:half], weight_gram[half:])


def window_phase(me, core, counts, weights, parts, mix):
    whole = pl.BlockSpec(memory_space=VMEM)
    smem = pl.BlockSpec(memory_space=SMEM)
    block = jax.ShapeDtypeStruct((CROWS, RANK), F32)
    half = jax.ShapeDtypeStruct((RANK // 2, 2 * RANK), F32)
    return pl.pallas_call(
        window_kernel,
        in_specs=[smem, smem, smem] + [whole] * 7,
        out_specs=[whole] * 4,
        out_shape=[block, block, half, half],
        compiler_params=pltpu.CompilerParams(vmem_limit_bytes=40 * 1024 * 1024),
        cost_estimate=pl.CostEstimate(flops=10**9, bytes_accessed=4 * 10**6, transcendentals=0),
    )(me, core, counts, weights, *parts, mix)


def tail_kernel(me_ref, counts_ref, sums_ref, cgram_ref, mix_ref, q_ref, proj_ref, weight_ref,
                mix_out, weight_out):
    me = me_ref[0]
    target = sums_ref[:, 0:RANK]
    code_gram = cgram_ref[...]
    curvature = sums_ref[:, RANK : 2 * RANK] * code_gram
    scale = jnp.sqrt(jnp.sum(curvature * curvature, keepdims=True))
    curved = split(curvature)
    mixing = mix_ref[...]
    for _ in range(NNLS_ITERS):
        mixing = jnp.maximum(mixing - (dot3(mixing, curved) - target) / scale, 0.0)
    mix_out[...] = mixing
    halves = split(mixing)
    second = dot3(halves, halves, 0, 0) * code_gram
    second_scale = jnp.sqrt(jnp.sum(second * second, keepdims=True))
    terms = []
    for i in range(CHUNK):
        rows = pl.ds(i * TILE, TILE)
        down, _ = patients_of(counts_ref, me * CHUNK + i)
        product = proj_ref[rows, :] * dot3(q_ref[rows, :], halves)
        for p in range(4):
            terms.append(jnp.sum(jnp.where(down == p, product, 0.0), axis=0, keepdims=True))
    terms = jnp.concatenate(terms, axis=0)
    seconds = split(second)
    weight = weight_ref[...]
    for _ in range(NNLS_ITERS):
        weight = jnp.maximum(weight - (dot3(weight, seconds) - terms) / second_scale, 0.0)
    for s in range(N_CODE):
        weight_out[s] = weight


def place_kernel(me_ref, q_ref, left_ref, right_ref, first_ref, second_ref, out_ref):
    half = CROWS // 2

    def put(step, rows, ref):
        @pl.when(pl.program_id(0) == step)
        def _():
            out_ref[rows, :] = ref[...]

    everything = pl.ds(0, CROWS)
    put(0, everything, q_ref)
    put(1, everything, left_ref)
    put(2, pl.ds(0, half), first_ref)
    put(2, pl.ds(half, half), second_ref)
    put(3, everything, right_ref)


def place(me, parts):
    return pl.pallas_call(
        place_kernel,
        grid_spec=pltpu.PrefetchScalarGridSpec(
            num_scalar_prefetch=1,
            grid=(N_CODE,),
            in_specs=[pl.BlockSpec(x.shape, lambda g, m: (0, 0)) for x in parts],
            out_specs=pl.BlockSpec((CROWS, RANK), lambda g, m: (lax.rem(m[0] + N_CODE - g, N_CODE), 0)),
        ),
        out_shape=jax.ShapeDtypeStruct((N_CODE * CROWS, RANK), F32),
        cost_estimate=pl.CostEstimate(flops=0, bytes_accessed=4 * 10**6, transcendentals=0),
    )(me, *parts)


def tail_phase(me, counts, sums, cgram, mix, q, proj, weights):
    whole = pl.BlockSpec(memory_space=VMEM)
    smem = pl.BlockSpec(memory_space=SMEM)
    return pl.pallas_call(
        tail_kernel,
        in_specs=[smem, smem] + [whole] * 6,
        out_specs=[whole, whole],
        out_shape=[
            jax.ShapeDtypeStruct((RANK, RANK), F32),
            jax.ShapeDtypeStruct((N_CODE, CHUNK * 4, RANK), F32),
        ],
        compiler_params=pltpu.CompilerParams(vmem_limit_bytes=SCOPED),
        cost_estimate=pl.CostEstimate(flops=10**9, bytes_accessed=4 * 10**6, transcendentals=0),
    )(me, counts, sums, cgram, mix, q, proj, weights)


def halves_of(x, p):
    half = x.shape[0] // 2
    return lax.dynamic_slice_in_dim(x, p * half, half, 0), lax.dynamic_slice_in_dim(x, (1 - p) * half, half, 0)


def join(mine, p):
    other = shift(mine, "pgroup", 2, 1)
    return jnp.where(p == 0, jnp.concatenate([mine, other], 0), jnp.concatenate([other, mine], 0))


def around_y(x, step):
    return lax.ppermute(x, "vrow", [(v, v // 4 * 4 + (v + step) % 4) for v in range(32)])


def local(tile_values, tile_block, visit_counts, code_factor, slice_mix, patient_weight):
    c = lax.axis_index("code")
    p = lax.axis_index("pgroup")
    y = lax.axis_index("vrow") % 4
    me = jnp.reshape(c, (1,)).astype(jnp.int32)
    windows = tile_block.shape[0]
    blocks = code_factor.shape[0] // TILE
    piece = code_factor.shape[0] // 8
    first = lax.dynamic_slice_in_dim(code_factor, (y * 2 + p) * piece, piece, 0)
    mine = shift(first, "code", N_CODE, 2)
    up_tiles, down_tiles = pack(me, tile_values, tile_block, first)
    down_tiles, mine = lax.optimization_barrier((down_tiles, mine))
    r1 = shift(up_tiles, "code", N_CODE, 1)
    r3 = shift(down_tiles, "code", N_CODE, 3)
    pieces = [mine] + [around_y(mine, s) for s in (1, 3, 2)]
    code_part = gram(code_factor, first)
    pieces, code_part = lax.optimization_barrier((pieces, code_part))
    pieces = pieces + [shift(x, "pgroup", 2, 1) for x in pieces]

    opposite = (c + 2) % N_CODE
    far_ids = lax.dynamic_slice_in_dim(tile_block, opposite * 2, 2, 1).reshape(-1) - opposite * blocks
    far_ids = jnp.clip(far_ids, 0, blocks - 1)
    per_piece = blocks // 8
    part = far_ids // per_piece
    behind = (y - part // 2) % 4
    behind = jnp.where(behind == 2, 3, jnp.where(behind == 3, 2, behind))
    far_ids = (jnp.where(part % 2 == p, 0, 4) + behind) * per_piece + far_ids % per_piece

    inputs = (me, tile_block, far_ids, tile_values, r1, r3, code_factor, pieces)
    far = project(*inputs, (2,))
    up = shift(far[0], "code", N_CODE, 1)
    down = shift(far[1], "code", N_CODE, 3)
    near = project(*inputs, (1, 3, 0))
    near, up, down = lax.optimization_barrier((near, up, down))
    right, right2, left, left2, kept = near
    from_left2 = shift(right2, "code", N_CODE, 1)
    from_right = shift(left, "code", N_CODE, 3)
    from_left = shift(right + up, "code", N_CODE, 1)
    from_right2 = shift(left2 + down, "code", N_CODE, 3)
    parts = (kept, from_left, from_left2, from_right, from_right2)

    my_weights = lax.dynamic_slice_in_dim(patient_weight, c * 16, 16, 0)
    core = jnp.reshape(p, (1,)).astype(jnp.int32)
    code_half = halves_of(code_part, p)[0]
    code_half = code_half + shift(code_half, "code", N_CODE, 2)
    parts, code_half = lax.optimization_barrier((parts, code_half))
    proj, q, sent, passed = window_phase(me, core, visit_counts, my_weights, parts, slice_mix)
    axes = ("code", "vrow")
    gathered = [shift(q, "code", N_CODE, s) for s in (1, 3)]
    sent = (sent + shift(passed, "pgroup", 2, 1))[:, None, :]
    row = jnp.sum(lax.all_to_all(sent, axes, 0, 0, tiled=True), axis=0)
    code_half = code_half + shift(code_half, "code", N_CODE, 1)
    row, gathered, code_half = lax.optimization_barrier((row, gathered, code_half))
    code_gram = join(code_half, p)
    half = CROWS // 2
    last = [shift(gathered[0][:half], "code", N_CODE, 1), shift(gathered[1][half:], "code", N_CODE, 3)]
    spread = jnp.broadcast_to(row[None], (RANK // 2,) + row.shape)
    back, last = lax.optimization_barrier((lax.all_to_all(spread, axes, 0, 0, tiled=True), last))
    sums = join(back[:, 0, :], p)
    mixing, spread = tail_phase(me, visit_counts, sums, code_gram, slice_mix, q, proj, my_weights)
    factor = place(me, [q, gathered[0], gathered[1]] + last)
    weight_new = lax.all_to_all(spread, "code", 0, 0, tiled=True).reshape(patient_weight.shape)
    return (factor, mixing, weight_new)


def solution(mesh):
    placed = (
        P(("pgroup", "vrow"), "code"),
        P(("pgroup", "vrow"), "code"),
        P(("pgroup", "vrow"), None),
        P("code", None),
        P(),
        P(("pgroup", "vrow"), None),
    )
    return jax.shard_map(
        local,
        mesh=mesh,
        in_specs=placed,
        out_specs=(P(("pgroup", "vrow"), None), P(), P(("pgroup", "vrow"), None)),
        check_vma=False,
    )
```
